256 devices in a mesh: dp: 4 (over y_hi, core), expert: 64 (over z, y_lo, x).
Axes of the slice: x: 4, y: 4 (y_hi: 2, y_lo: 2; y = y_hi * 2 + y_lo), z: 8, core: 2. Of those that a mesh axis runs over, the one named last changes fastest.
Arguments:
- tokens: bfloat16 [8192, 4096], P('expert', 'dp'), may hold values from -6 to 6
- cotangent: bfloat16 [8192, 4096], P('expert', 'dp'), may hold values from -6 to 6
- routes: int32 [8192, 8], P('expert'), may hold values from 0 to 63, all different within a row; in each aligned block of 128 rows (0 to 127, 128 to 255, ...) at most 18 rows name the same one
- router: bfloat16 [64, 4096], P(None, 'dp'), may hold values from -0.1875 to 0.1875
- w_gate: bfloat16 [64, 4096, 768], P('expert', 'dp'), may hold values from -0.09375 to 0.09375
- w_up: bfloat16 [64, 4096, 768], P('expert', 'dp'), may hold values from -0.09375 to 0.09375
- w_down: bfloat16 [64, 768, 4096], P('expert', None, 'dp'), may hold values from -0.21875 to 0.21875
Outputs:
- grad_tokens: bfloat16 [8192, 4096], P('expert', 'dp')
- grad_gate: bfloat16 [64, 4096, 768], P('expert', 'dp')
- grad_up: bfloat16 [64, 4096, 768], P('expert', 'dp')
- grad_down: bfloat16 [64, 768, 4096], P('expert', None, 'dp')
- grad_router: float32 [64, 4096], P(None, 'dp')
The draws below stay inside these ranges and needn't reach their ends.
Inputs may be any that keep to these rules, and one draw needn't show every extreme that they name: `routes`: each row names 8 different experts. Within each aligned block of 128 rows no expert is named by more than 18 rows, and in some block an expert is named by exactly 18 rows.
All inputs are finite; a program needn't handle non-finite values.
Results may differ from the reference program's by a relative error of at most 0.039.
Values may be sent and summed in bfloat16 or wider, within the bound.
No kernel may reach another device: no remote copies, remote signals or barrier semaphores. Data moves between devices by JAX's collectives and lax.ppermute only.
A program may use at most 128 MiB of HBM per device.

```python
import math
import jax
import jax.numpy as jnp
import numpy as np
from jax import lax

D = 4096
FF = 768
TOP = 8
TOK_DEV = 128
EXPERTS = 64
TOKENS = 8192
CAP = 18
N_DP = 4
N_EXPERT = 64


def block_scale(own_key, extent, shards, smallest, high):
    factor_of, own = 1.0, jax.random.fold_in(own_key, 6)
    for position, parts in shards:
        steps = jnp.exp(jax.random.uniform(jax.random.fold_in(own, position), (parts,), jnp.float32, smallest / len(shards), high / len(shards)))
        factor_of = factor_of * jnp.repeat(steps, extent[position] // parts).reshape([-1 if axis == position else 1 for axis in range(len(extent))])
    return factor_of


def routed_block(key, own, number, rows, count, top, limit, lean):
    order = jax.random.permutation(key, count)
    heavy_load, ordinary = portions_of(count, rows * top, limit, lean, True), portions_of(count, rows * top, limit, lean, False)
    places = jnp.arange(count)

    def named(sizes, offset_by):
        used = int((sizes > 0).sum())
        fixed = max(1, used // 4)
        moved = fixed + (places - fixed + offset_by * (used - fixed)) % max(1, count - fixed)
        return jnp.zeros((count,), jnp.int32).at[order[jnp.where(places < fixed, places, moved)]].set(jnp.asarray(sizes, jnp.int32))

    sizes = jnp.where(number % 4 == 0, named(heavy_load, number // 4), named(ordinary, number - number // 4 - 1))
    mixed = jax.random.permutation(jax.random.fold_in(own, 3), count)
    donor, sink = mixed[0:count // 2 * 2:2], mixed[1:count // 2 * 2:2]
    slack = jnp.minimum(sizes[donor] - 1, limit - sizes[sink]) // 2
    slack = jnp.where((donor == order[0]) | (sink == order[0]) | (sizes[sink] == 0), 0, jnp.maximum(slack, 0))
    moved = jax.random.randint(jax.random.fold_in(own, 4), (count // 2,), 0, 1 << 20) % (slack + 1)
    sizes = sizes.at[donor].add(-moved).at[sink].add(moved)
    items = jnp.searchsorted(jnp.cumsum(sizes), jnp.arange(rows * top), side="right").astype(jnp.int32)
    grid = items.reshape(top, rows).T
    grid = grid[jax.random.permutation(jax.random.fold_in(own, 1), rows)]
    offset_by = jax.random.randint(jax.random.fold_in(own, 2), (rows, 1), 0, top)
    return jnp.take_along_axis(grid, (jnp.arange(top)[None, :] + offset_by) % top, axis=1)


def portions_of(amount, total, limit, skew, full):
    weights = [(1 << 20) // math.isqrt(grade ** skew) + 1 for grade in range(1, amount + 1)]
    largest = limit if full else min(limit, max(-(-total // amount), total * weights[0] // sum(weights)))
    least = 1 if total - largest >= amount - 1 else 0
    counts, spare = [largest] + [least] * (amount - 1), total - largest - least * (amount - 1)
    while spare > 0:
        movable = [i for i in range(1, amount) if counts[i] < largest] or [i for i in range(1, amount) if counts[i] < limit]
        mass, left = sum([weights[i] for i in movable]), spare
        for i in movable:
            extra = min(limit - counts[i], max(1, left * weights[i] // mass), spare)
            counts[i] = counts[i] + extra
            spare = spare - extra
    return np.array(counts)


def bell_draw(own_key, shape, spread, bound, split=(), held_as=jnp.bfloat16):
    result = spread * jax.random.normal(own_key, shape, jnp.float32)
    if split:
        result = result * block_scale(own_key, shape, split, -0.22, 0.18)
    return jnp.clip(result, -bound, bound).astype(held_as)


def setup_inputs(seed: int = 0) -> dict:
    splits = jax.random.split(jax.random.key(seed), 8)
    tokens = bell_draw(splits[0], (TOKENS, D), 1.0, 6.0, ((0, 64), (1, 4)))
    cotangent = bell_draw(splits[1], (TOKENS, D), 1.0, 6.0, ((0, 64), (1, 4)))
    routes_keys = jax.random.split(jax.random.fold_in(splits[2], 1), TOKENS // TOK_DEV)
    routes_turns = jax.random.permutation(jax.random.fold_in(splits[2], 3), TOKENS // TOK_DEV)
    routes = jax.vmap(lambda own, number: routed_block(jax.random.fold_in(splits[2], 2), own, number, TOK_DEV, EXPERTS, TOP, CAP, 1))(routes_keys, routes_turns).reshape((TOKENS, TOP))
    router = bell_draw(splits[3], (EXPERTS, D), (D // 4) ** -0.5, 0.1875, ((1, 4),))
    w_gate = bell_draw(splits[4], (EXPERTS, D, FF), D ** -0.5, 0.09375, ((0, 64), (1, 4)))
    w_up = bell_draw(splits[5], (EXPERTS, D, FF), D ** -0.5, 0.09375, ((0, 64), (1, 4)))
    w_down = bell_draw(splits[6], (EXPERTS, FF, D), FF ** -0.5, 0.21875, ((0, 64), (2, 4)))
    return dict(tokens=tokens, cotangent=cotangent, routes=routes, router=router, w_gate=w_gate, w_up=w_up, w_down=w_down)


def range_sum(left_rows, right_cols, form):
    slot_rows = left_rows.shape[0]
    columns = D // N_DP
    left_part = left_rows.reshape(slot_rows, N_DP, columns).astype(jnp.float32)
    partial_terms = jnp.einsum(form, left_part, right_cols.astype(jnp.float32))
    rounded = lax.optimization_barrier(partial_terms.astype(jnp.bfloat16))
    return jnp.sum(rounded.astype(jnp.float32), axis=0)


def reference(tokens, cotangent, routes, router, w_gate, w_up, w_down):
    columns = D // N_DP
    slot_rows = N_EXPERT * CAP
    pair_count = TOKENS * TOP
    logits = jnp.dot(tokens, router.T, preferred_element_type=jnp.float32)
    labels = jnp.arange(EXPERTS, dtype=jnp.int32)
    onehot = routes[:, :, None] == labels
    selected = jnp.sum(jnp.where(onehot, logits[:, None, :], jnp.float32(0.0)), axis=2)
    exponent = jnp.exp(selected)
    weights = exponent / jnp.sum(exponent, axis=1, keepdims=True)
    blocks = routes.reshape(N_EXPERT, TOK_DEV * TOP)
    expert_flags = (blocks[:, :, None] == labels).astype(jnp.int32)
    earlier = jnp.cumsum(expert_flags, axis=1) - expert_flags
    slot_index = jnp.sum(earlier * expert_flags, axis=2).astype(jnp.int32)
    pair_ids = jnp.arange(pair_count, dtype=jnp.int32).reshape(N_EXPERT, TOK_DEV * TOP)
    block_ids = jnp.broadcast_to(jnp.arange(N_EXPERT, dtype=jnp.int32)[:, None], blocks.shape)
    source_pair = jnp.full((EXPERTS, N_EXPERT, CAP), pair_count, jnp.int32)
    source_pair = source_pair.at[blocks, block_ids, slot_index].set(pair_ids).reshape(EXPERTS, slot_rows)
    token_pad = jnp.concatenate([tokens, jnp.zeros((1, D), jnp.bfloat16)], axis=0)
    cotangent_pad = jnp.concatenate([cotangent, jnp.zeros((1, D), jnp.bfloat16)], axis=0)
    weight_pad = jnp.concatenate([weights.reshape(-1), jnp.zeros((1,), jnp.float32)])

    def one_expert(running, inputs):
        grad_sum, score_sum = running
        pair_index, gate_matrix, up_matrix, down_matrix = inputs
        source_token = (pair_index // TOP).astype(jnp.int32)
        recv_tokens = token_pad[source_token]
        recv_grads = (weight_pad[pair_index][:, None] * cotangent_pad[source_token].astype(jnp.float32)).astype(jnp.bfloat16)
        gate_value = range_sum(recv_tokens, gate_matrix.reshape(N_DP, columns, FF), "rsd,sdf->srf")
        up_value = range_sum(recv_tokens, up_matrix.reshape(N_DP, columns, FF), "rsd,sdf->srf")
        sigmoid_gate = jax.nn.sigmoid(gate_value)
        hidden = (gate_value * sigmoid_gate * up_value).astype(jnp.bfloat16)
        hidden_grad = range_sum(recv_grads, down_matrix.reshape(FF, N_DP, columns), "rsd,fsd->srf")
        route_score = jnp.sum(hidden_grad * hidden.astype(jnp.float32), axis=1).astype(jnp.bfloat16)
        grad_down = jnp.dot(hidden.T, recv_grads, preferred_element_type=jnp.float32).astype(jnp.bfloat16)
        gate_grad = (hidden_grad * up_value * sigmoid_gate * (1.0 + gate_value * (1.0 - sigmoid_gate))).astype(jnp.bfloat16)
        up_grad = (hidden_grad * gate_value * sigmoid_gate).astype(jnp.bfloat16)
        grad_gate = jnp.dot(recv_tokens.T, gate_grad, preferred_element_type=jnp.float32).astype(jnp.bfloat16)
        grad_up = jnp.dot(recv_tokens.T, up_grad, preferred_element_type=jnp.float32).astype(jnp.bfloat16)
        token_grads = (jnp.dot(gate_grad, gate_matrix.T, preferred_element_type=jnp.float32)
                       + jnp.dot(up_grad, up_matrix.T, preferred_element_type=jnp.float32)).astype(jnp.bfloat16)
        grad_sum = grad_sum.at[source_token].add(token_grads.astype(jnp.float32))
        score_sum = score_sum.at[pair_index].set(route_score.astype(jnp.float32))
        return (grad_sum, score_sum), (grad_gate, grad_up, grad_down)

    start = (jnp.zeros((TOKENS + 1, D), jnp.float32), jnp.zeros((pair_count + 1,), jnp.float32))
    (grad_sum, score_sum), (grad_gate, grad_up, grad_down) = lax.scan(
        one_expert, start, (source_pair, w_gate, w_up, w_down))
    pair_score = score_sum[:pair_count].reshape(TOKENS, TOP)
    select_grad = pair_score - weights * jnp.sum(pair_score, axis=1, keepdims=True)
    logit_grad = jnp.sum(jnp.where(onehot, select_grad[:, :, None], jnp.float32(0.0)), axis=1).astype(jnp.bfloat16)
    grad_tokens = (grad_sum[:TOKENS] + jnp.dot(logit_grad, router, preferred_element_type=jnp.float32)).astype(jnp.bfloat16)
    grad_router = jnp.dot(logit_grad.T, tokens, preferred_element_type=jnp.float32)
    return grad_tokens, grad_gate, grad_up, grad_down, grad_router
```

```python
import jax
import jax.numpy as jnp
from jax import lax
from jax.sharding import Mesh, PartitionSpec as P

BF = jnp.bfloat16
F32 = jnp.float32
NZ = 8
NPLANE = 8
DP = ("yh", "c")
EXPERT = ("z", "yl", "x")
PLANE = ("yl", "x")


def dot(a, b, da, db):
    return lax.dot_general(a, b, (((da,), (db,)), ((), ())), preferred_element_type=F32)


def shift(n, k):
    return [(i, (i + k) % n) for i in range(n)]


def swap(a, axis):
    return lax.ppermute(a, axis, [(0, 1), (1, 0)])


def exchange(a, axis):
    return lax.all_to_all(a, axis, split_axis=0, concat_axis=0, tiled=True)


def ring_gather(block, zi, parts):
    rows, columns = block.shape
    width = columns // parts
    pieces = [block[:, j * width : (j + 1) * width] for j in range(parts)]
    outs = [lax.dynamic_update_slice(jnp.zeros((NZ, rows, width), BF), p[None], (zi, 0, 0)) for p in pieces]
    right, left = list(pieces), list(pieces)
    for i in range(1, NZ // 2 + 1):
        for j in range(parts):
            right[j] = lax.ppermute(right[j], "z", shift(NZ, 1))
            outs[j] = lax.dynamic_update_slice(outs[j], right[j][None], ((zi - i) % NZ, 0, 0))
            if i < NZ // 2:
                left[j] = lax.ppermute(left[j], "z", shift(NZ, -1))
                outs[j] = lax.dynamic_update_slice(outs[j], left[j][None], ((zi + i) % NZ, 0, 0))
    return jnp.concatenate([o.reshape(NZ * rows, width) for o in outs], axis=1)


def ring_reduce(blocks, zi):
    def term(offset):
        return lax.dynamic_index_in_dim(blocks, (zi + offset) % NZ, 0, keepdims=False)

    right, left = term(4), term(-3)
    for i in range(4):
        right = lax.ppermute(right, "z", shift(NZ, 1))
        if i < 3:
            right = (right.astype(F32) + term(3 - i).astype(F32)).astype(BF)
            left = lax.ppermute(left, "z", shift(NZ, -1))
            if i < 2:
                left = (left.astype(F32) + term(i - 2).astype(F32)).astype(BF)
    return (term(0).astype(F32) + right.astype(F32) + left.astype(F32)).astype(BF)


def per_device(tokens, cotangent, routes, router, w_gate, w_up, w_down):
    rows, columns = tokens.shape
    experts = router.shape[0]
    capacity = 9 * rows * routes.shape[1] // (8 * experts)
    quota = NZ * capacity
    slots = NPLANE * quota
    half = slots // 2
    zi, ci = lax.axis_index("z"), lax.axis_index("c")
    w_gate, w_up, w_down = w_gate[0], w_up[0], w_down[0]

    cot_all = lax.all_gather(cotangent, "z", axis=0, tiled=True)
    tok_all = ring_gather(tokens, zi, 2)

    logit_part = dot(router, tokens, 1, 1).astype(BF)
    logits = jnp.sum(lax.all_gather(logit_part, DP, axis=0).astype(F32), axis=0)
    labels = lax.broadcasted_iota(jnp.int32, (experts, rows), 0)
    named = jnp.any(routes.T[:, None, :] == labels[None], axis=0)
    exponent = jnp.where(named, jnp.exp(logits), 0.0)
    weight = exponent / jnp.sum(exponent, axis=0, keepdims=True)
    before = (
        lax.broadcasted_iota(jnp.int32, (rows, rows), 0) < lax.broadcasted_iota(jnp.int32, (rows, rows), 1)
    ).astype(BF)
    slot = dot(named.astype(BF), before, 1, 0)
    place = jnp.where(named, slot + (zi * capacity).astype(F32), -1.0)
    packed = jnp.concatenate(
        [place.reshape(NZ, NPLANE, rows), weight.reshape(NZ, NPLANE, rows)], axis=1
    )
    packed = exchange(packed, "z")
    packed = jnp.swapaxes(packed, 0, 1).reshape(2 * NPLANE, NZ * rows)
    place, weight = packed[:NPLANE], packed[NPLANE:]
    hit = place[:, None, :] == lax.broadcasted_iota(jnp.int32, (1, quota, 1), 1).astype(F32)
    select = hit.astype(BF).reshape(slots, NZ * rows)
    slot_weight = jnp.sum(jnp.where(hit, weight[:, None, :], 0.0), axis=2).reshape(slots, 1)

    send_tok = dot(select, tok_all, 1, 0).astype(BF)
    xr = exchange(send_tok.reshape(NPLANE, quota, columns), PLANE).reshape(slots, columns)
    send_cot = (slot_weight * dot(select, cot_all, 1, 0)).astype(BF)
    dyw = exchange(send_cot.reshape(NPLANE, quota, columns), PLANE).reshape(slots, columns)

    def own(a):
        return lax.dynamic_slice_in_dim(a, ci * half, half, 0)

    def other(a):
        return lax.dynamic_slice_in_dim(a, (1 - ci) * half, half, 0)

    def total(a, b, db):
        away = swap(dot(other(a), b, 1, db).astype(BF), "c")
        here = dot(own(a), b, 1, db).astype(BF)
        pair = (here.astype(F32) + away.astype(F32)).astype(BF)
        return pair.astype(F32) + swap(pair, "yh").astype(F32)

    gate = total(xr, w_gate, 0)
    up = total(xr, w_up, 0)
    dh = total(dyw, w_down, 1)
    sig = jax.nn.sigmoid(gate)
    hidden = (gate * sig * up).astype(BF)
    score = jnp.sum(dh * hidden.astype(F32), axis=1).astype(BF)
    gate_grad = (dh * up * sig * (1.0 + gate * (1.0 - sig))).astype(BF)
    up_grad = (dh * gate * sig).astype(BF)

    def whole(a):
        b = swap(a, "c")
        first = ci == 0
        return jnp.concatenate([jnp.where(first, a, b), jnp.where(first, b, a)], axis=0)

    score = whole(score)
    gate_grad = whole(gate_grad)
    up_grad = whole(up_grad)
    hidden = whole(hidden)

    back = (dot(gate_grad, w_gate, 1, 1) + dot(up_grad, w_up, 1, 1)).astype(BF)
    back = exchange(back.reshape(NPLANE, quota, columns), PLANE).reshape(slots, columns)
    score = exchange(score.astype(F32).reshape(NPLANE, 1, quota), PLANE).reshape(NPLANE, quota)
    pair_score = jnp.sum(jnp.where(hit, score[:, :, None], 0.0), axis=1)
    row_sum = jnp.sum(pair_score, axis=0).reshape(1, NZ, rows)
    row_sum = jnp.sum(exchange(jnp.broadcast_to(row_sum, (NZ, NZ, rows)), "z"), axis=0).reshape(1, NZ * rows)
    logit_grad = (pair_score - weight * row_sum).astype(BF)

    plane_router = lax.dynamic_slice_in_dim(router, zi * NPLANE, NPLANE, 0)
    partial = (dot(select, back, 0, 0) + dot(logit_grad, plane_router, 0, 0)).astype(BF)
    grad_tokens = ring_reduce(partial.reshape(NZ, rows, columns), zi)

    router_part = dot(logit_grad, tok_all, 1, 0)
    router_part = jnp.sum(
        exchange(jnp.broadcast_to(router_part[None], (NPLANE, NPLANE, columns)), PLANE), axis=0
    )
    grad_router = exchange(jnp.broadcast_to(router_part[None], (NZ, NPLANE, columns)), "z").reshape(
        experts, columns
    )

    grad_gate = dot(xr, gate_grad, 0, 0).astype(BF)
    grad_up = dot(xr, up_grad, 0, 0).astype(BF)
    grad_down = dot(hidden, dyw, 0, 0).astype(BF)
    return grad_tokens, grad_gate[None], grad_up[None], grad_down[None], grad_router


def solution(mesh):
    fine = Mesh(mesh.devices.reshape(2, 2, NZ, 2, 4), DP + EXPERT)
    in_specs = (
        P(EXPERT, DP),
        P(EXPERT, DP),
        P(EXPERT, None),
        P(None, DP),
        P(EXPERT, DP, None),
        P(EXPERT, DP, None),
        P(EXPERT, None, DP),
    )
    out_specs = (
        P(EXPERT, DP),
        P(EXPERT, DP, None),
        P(EXPERT, DP, None),
        P(EXPERT, None, DP),
        P(None, DP),
    )
    return jax.shard_map(
        per_device, mesh=fine, in_specs=in_specs, out_specs=out_specs, check_vma=False
    )
```

```python
import jax
import jax.numpy as jnp
from jax import lax
from jax.sharding import Mesh, PartitionSpec as P

BF = jnp.bfloat16
F32 = jnp.float32
NZ = 8
NPLANE = 8
MORE = 16
DP = ("yh", "c")
EXPERT = ("z", "yl", "x")
PLANE = ("x", "yl")


def dot(a, b, da, db):
    return lax.dot_general(a, b, (((da,), (db,)), ((), ())), preferred_element_type=F32)


def shift(n, k):
    return [(i, (i + k) % n) for i in range(n)]


def swap(a, axis):
    return lax.ppermute(a, axis, [(0, 1), (1, 0)])


def exchange(a, axis):
    return lax.all_to_all(a, axis, split_axis=0, concat_axis=0, tiled=True)


def ring_gather(block, extra, zi, parts, late):
    rows, columns = block.shape
    width = columns // parts
    whole = (jnp.zeros((NZ, rows, columns), BF), jnp.zeros((NZ, extra.shape[0], columns), BF))

    def keep(out, part, at, j):
        return (
            lax.dynamic_update_slice(out[0], part[None, :rows], (at, 0, j * width)),
            lax.dynamic_update_slice(out[1], part[None, rows:], (at, 0, j * width)),
        )

    cut = [slice(j * width, (j + 1) * width) for j in range(parts)]
    right = [jnp.concatenate([block[:, c], extra[:, c]], axis=0) for c in cut]
    left = list(right)
    for j in range(parts):
        whole = keep(whole, right[j], zi, j)
    for i in range(1, NZ // 2 + 1):
        if i == late:
            passed = right[0]
        for j in range(parts):
            right[j] = lax.ppermute(right[j], "z", shift(NZ, 1))
            whole = keep(whole, right[j], (zi - i) % NZ, j)
            if i < NZ // 2:
                left[j] = lax.ppermute(left[j], "z", shift(NZ, -1))
                whole = keep(whole, left[j], (zi + i) % NZ, j)
    return whole[0].reshape(NZ * rows, columns), whole[1], passed


def per_device(tokens, cotangent, routes, router, w_gate, w_up, w_down):
    rows, columns = tokens.shape
    experts = router.shape[0]
    capacity = 9 * rows * routes.shape[1] // (8 * experts)
    quota = NZ * capacity
    slots = NPLANE * quota
    half = slots // 2
    zi, yi, ci = lax.axis_index("z"), lax.axis_index("yl"), lax.axis_index("c")
    w_gate, w_up, w_down = w_gate[0], w_up[0], w_down[0]

    def in_order(own_part, other_part):
        first = yi == 0
        return jnp.stack([jnp.where(first, own_part, other_part), jnp.where(first, other_part, own_part)])

    def turned(a, count):
        return jnp.swapaxes(a.reshape(count, -1, *a.shape[1:]), 0, 1).reshape(a.shape)

    labels = lax.broadcasted_iota(jnp.int32, (experts, rows), 0)
    named = jnp.any(routes.T[:, None, :] == labels[None], axis=0)
    before = (
        lax.broadcasted_iota(jnp.int32, (rows, rows), 0) < lax.broadcasted_iota(jnp.int32, (rows, rows), 1)
    ).astype(BF)
    slot = jnp.where(named, dot(named.astype(BF), before, 1, 0), -1.0).astype(BF)
    slot = slot.reshape(NZ, NPLANE * rows)

    tok_all, slot_all, passed = ring_gather(tokens, slot, zi, 2, 3)
    cot_pair = in_order(cotangent, swap(cotangent, "yl"))
    cot_pair, _ = lax.optimization_barrier((cot_pair, passed))
    cot_all = lax.all_gather(cot_pair, "z", axis=1, tiled=True)
    slot_all = slot_all.astype(F32)
    offset = lax.broadcasted_iota(jnp.int32, (NZ, 1, 1), 0).astype(F32) * capacity
    place = lax.dynamic_slice_in_dim(slot_all, zi, 1, 1).reshape(NZ, NPLANE, rows)
    place = jnp.where(place >= 0.0, place + offset, -1.0)
    place = turned(jnp.swapaxes(place, 0, 1).reshape(NPLANE, NZ * rows), 2)

    def hits(q, place=place):
        return place[..., None, :] == lax.broadcasted_iota(jnp.int32, (1, q, 1), 1).astype(F32)

    hit = hits(quota)
    select = hit.astype(BF).reshape(slots, NZ * rows)

    run = NPLANE // 2

    def part(at):
        return lax.dynamic_index_in_dim(place.reshape(run, 2, -1), at, 1, keepdims=False)

    both = in_order(part(yi), swap(part(1 - yi), "yl"))

    send_tok = dot(select, tok_all, 1, 0).astype(BF)
    send_tok, both = lax.optimization_barrier((send_tok, both))
    xr = exchange(send_tok.reshape(NPLANE, quota, columns), PLANE).reshape(slots, columns)

    score_part = dot(router, tok_all, 1, 1)
    pair_part = (score_part + swap(score_part, "c")).astype(BF)
    logits = pair_part.astype(F32) + swap(pair_part, "yh").astype(F32)
    named_all = jnp.swapaxes(slot_all.reshape(NZ, experts, rows), 0, 1).reshape(experts, NZ * rows) >= 0.0
    exponent = jnp.where(named_all, jnp.exp(logits), 0.0)
    weight_all = exponent / jnp.sum(exponent, axis=0, keepdims=True)
    weight = turned(lax.dynamic_slice_in_dim(weight_all, zi * NPLANE, NPLANE, 0), 2)
    slot_weight = jnp.sum(jnp.where(hit, weight[:, None, :], 0.0), axis=2)

    select2 = hits(quota, both).astype(BF).reshape(2, run * quota, NZ * rows)
    send_cot = lax.dot_general(select2, cot_all, (((2,), (1,)), ((0,), (0,))), preferred_element_type=F32)
    send_cot = jnp.swapaxes(send_cot.astype(BF).reshape(2, run, quota, columns), 0, 1)
    xr, send_cot = lax.optimization_barrier((xr, send_cot))
    raw = exchange(send_cot, "x").reshape(slots, columns)
    def own(a):
        return lax.dynamic_slice_in_dim(a, ci * half, half, 0)

    def other(a):
        return lax.dynamic_slice_in_dim(a, (1 - ci) * half, half, 0)

    def pair_sum(a, b, db):
        away = swap(dot(other(a), b, 1, db).astype(BF), "c")
        here = dot(own(a), b, 1, db).astype(BF)
        return (here.astype(F32) + away.astype(F32)).astype(BF)

    def swapped(pair):
        return pair, swap(pair, "yh")

    def total(pair):
        return pair[0].astype(F32) + pair[1].astype(F32)

    gate = pair_sum(xr, w_gate, 0)
    up = pair_sum(xr, w_up, 0)
    gate = swapped(gate)
    raw, gate, up = lax.optimization_barrier((raw, gate, up))
    up = swapped(up)
    dh = pair_sum(raw, w_down, 1)
    dh, up, slot_weight = lax.optimization_barrier((dh, up, slot_weight))
    slot_weight = exchange(slot_weight.reshape(NPLANE, 1, quota), PLANE).reshape(slots, 1)
    gate, up, dh = total(gate), total(up), own(slot_weight) * total(swapped(dh))
    sig = jax.nn.sigmoid(gate)
    hidden = (gate * sig * up).astype(BF)
    score = jnp.sum(dh * hidden.astype(F32), axis=1).astype(BF)
    gate_grad = (dh * up * sig * (1.0 + gate * (1.0 - sig))).astype(BF)
    up_grad = (dh * gate * sig).astype(BF)

    def whole(a):
        b = swap(a, "c")
        first = ci == 0
        return jnp.concatenate([jnp.where(first, a, b), jnp.where(first, b, a)], axis=0)

    gate_grad, up_grad, score, hidden = (whole(a) for a in (gate_grad, up_grad, score, hidden))

    back = (dot(gate_grad, w_gate, 1, 1) + dot(up_grad, w_up, 1, 1)).astype(BF)
    score = jnp.pad(score.reshape(NPLANE, 1, quota), ((0, 0), (0, MORE - 1), (0, columns - quota)))
    back = jnp.concatenate([back.reshape(NPLANE, quota, columns), score], axis=1)
    back = exchange(back, PLANE)
    grad_gate = dot(xr, gate_grad, 0, 0).astype(BF)
    grad_up = dot(xr, up_grad, 0, 0).astype(BF)
    dyw = (slot_weight * raw.astype(F32)).astype(BF)
    grad_down = dot(hidden, dyw, 0, 0).astype(BF)
    back, grad_gate, grad_up, grad_down = lax.optimization_barrier((back, grad_gate, grad_up, grad_down))
    score = back[:, quota, :quota].astype(F32)
    back = back.reshape(NPLANE * (quota + MORE), columns)
    select_back = hits(quota + MORE).astype(BF).reshape(NPLANE * (quota + MORE), NZ * rows)
    partial = dot(select_back, back, 0, 0).astype(BF)

    pair_score = jnp.sum(jnp.where(hit, score[:, :, None], 0.0), axis=1)
    row_sum = jnp.sum(pair_score, axis=0).reshape(1, NZ, rows)
    packed = jnp.concatenate(
        [
            jnp.swapaxes(pair_score.reshape(NPLANE, NZ, rows), 0, 1),
            jnp.broadcast_to(row_sum, (NZ, NZ, rows)),
        ],
        axis=1,
    )
    packed = exchange(packed, "z")
    own_score = jnp.swapaxes(packed[:, :NPLANE].reshape(NZ, run, 2, rows), 1, 2).reshape(experts, rows)
    own_weight = lax.dynamic_slice_in_dim(weight_all, zi * rows, rows, 1)
    own_grad = (own_score - own_weight * jnp.sum(own_score, axis=0, keepdims=True)).astype(BF)
    row_sum = jnp.sum(packed[:, NPLANE:], axis=0).reshape(1, NZ * rows)
    logit_grad = (pair_score - weight * row_sum).astype(BF)

    router_part = dot(logit_grad, tok_all, 1, 0)
    router_part = jnp.sum(
        exchange(jnp.broadcast_to(router_part[None], (NPLANE, NPLANE, columns)), PLANE), axis=0
    )
    router_part = turned(router_part, run)
    grad_router = exchange(jnp.broadcast_to(router_part[None], (NZ, NPLANE, columns)), "z").reshape(
        experts, columns
    )
    grad_tokens = lax.psum_scatter(partial, "z", scatter_dimension=0, tiled=True)
    grad_tokens = (grad_tokens.astype(F32) + dot(own_grad, router, 0, 0)).astype(BF)

    return grad_tokens, grad_gate[None], grad_up[None], grad_down[None], grad_router


def solution(mesh):
    fine = Mesh(mesh.devices.reshape(2, 2, NZ, 2, 4), DP + EXPERT)
    in_specs = (
        P(EXPERT, DP),
        P(EXPERT, DP),
        P(EXPERT, None),
        P(None, DP),
        P(EXPERT, DP, None),
        P(EXPERT, DP, None),
        P(EXPERT, None, DP),
    )
    out_specs = (
        P(EXPERT, DP),
        P(EXPERT, DP, None),
        P(EXPERT, DP, None),
        P(EXPERT, None, DP),
        P(None, DP),
    )
    return jax.shard_map(
        per_device, mesh=fine, in_specs=in_specs, out_specs=out_specs, check_vma=False
    )
```

```python
import jax
import jax.numpy as jnp
from jax import lax
from jax.sharding import Mesh, PartitionSpec as P

BF = jnp.bfloat16
F32 = jnp.float32
NZ = 8
NPLANE = 8
MORE = 8
DP = ("yh", "c")
EXPERT = ("z", "yl", "x")
PLANE = ("x", "yl")


def dot(a, b, da, db):
    return lax.dot_general(a, b, (((da,), (db,)), ((), ())), preferred_element_type=F32)


def shift(n, k):
    return [(i, (i + k) % n) for i in range(n)]


def swap(a, axis):
    return lax.ppermute(a, axis, [(0, 1), (1, 0)])


def exchange(a, axis):
    return lax.all_to_all(a, axis, split_axis=0, concat_axis=0, tiled=True)


def ring_gather(block, extra, zi, parts, late):
    rows, columns = block.shape
    width = columns // parts
    whole = (jnp.zeros((NZ, rows, columns), BF), jnp.zeros((NZ, extra.shape[0], columns), BF))

    def keep(out, part, at, j):
        return (
            lax.dynamic_update_slice(out[0], part[None, :rows], (at, 0, j * width)),
            lax.dynamic_update_slice(out[1], part[None, rows:], (at, 0, j * width)),
        )

    cut = [slice(j * width, (j + 1) * width) for j in range(parts)]
    right = [jnp.concatenate([block[:, c], extra[:, c]], axis=0) for c in cut]
    left = list(right)
    for j in range(parts):
        whole = keep(whole, right[j], zi, j)
    for i in range(1, NZ // 2 + 1):
        if i == late:
            passed = right[0]
        for j in range(parts):
            right[j] = lax.ppermute(right[j], "z", shift(NZ, 1))
            whole = keep(whole, right[j], (zi - i) % NZ, j)
            if i < NZ // 2:
                left[j] = lax.ppermute(left[j], "z", shift(NZ, -1))
                whole = keep(whole, left[j], (zi + i) % NZ, j)
    return whole[0].reshape(NZ * rows, columns), whole[1], passed


def per_device(tokens, cotangent, routes, router, w_gate, w_up, w_down):
    rows, columns = tokens.shape
    experts = router.shape[0]
    capacity = 9 * rows * routes.shape[1] // (8 * experts)
    quota = NZ * capacity
    slots = NPLANE * quota
    half = slots // 2
    zi, yi, ci = lax.axis_index("z"), lax.axis_index("yl"), lax.axis_index("c")
    w_gate, w_up, w_down = w_gate[0], w_up[0], w_down[0]

    def in_order(own_part, other_part):
        first = yi == 0
        return jnp.stack([jnp.where(first, own_part, other_part), jnp.where(first, other_part, own_part)])

    def turned(a, count):
        return jnp.swapaxes(a.reshape(count, -1, *a.shape[1:]), 0, 1).reshape(a.shape)

    labels = lax.broadcasted_iota(jnp.int32, (experts, rows), 0)
    named = jnp.any(routes.T[:, None, :] == labels[None], axis=0)
    before = (
        lax.broadcasted_iota(jnp.int32, (rows, rows), 0) < lax.broadcasted_iota(jnp.int32, (rows, rows), 1)
    ).astype(BF)
    slot = jnp.where(named, dot(named.astype(BF), before, 1, 0), -1.0).astype(BF)
    slot = slot.reshape(NZ, NPLANE * rows)

    tok_all, slot_all, passed = ring_gather(tokens, slot, zi, 2, 3)
    cot_pair = in_order(cotangent, swap(cotangent, "yl"))
    cot_pair, _ = lax.optimization_barrier((cot_pair, passed))
    cot_all = lax.all_gather(cot_pair, "z", axis=1, tiled=True)
    slot_all = slot_all.astype(F32)
    offset = lax.broadcasted_iota(jnp.int32, (NZ, 1, 1), 0).astype(F32) * capacity
    place = lax.dynamic_slice_in_dim(slot_all, zi, 1, 1).reshape(NZ, NPLANE, rows)
    place = jnp.where(place >= 0.0, place + offset, -1.0)
    place = turned(jnp.swapaxes(place, 0, 1).reshape(NPLANE, NZ * rows), 2)

    def hits(q, place=place):
        return place[..., None, :] == lax.broadcasted_iota(jnp.int32, (1, q, 1), 1).astype(F32)

    hit = hits(quota)
    select = hit.astype(BF).reshape(slots, NZ * rows)

    run = NPLANE // 2

    def part(at):
        return lax.dynamic_index_in_dim(place.reshape(run, 2, -1), at, 1, keepdims=False)

    both = in_order(part(yi), swap(part(1 - yi), "yl"))

    send_tok = dot(select, tok_all, 1, 0).astype(BF)
    send_tok, both = lax.optimization_barrier((send_tok, both))
    xr = exchange(send_tok.reshape(NPLANE, quota, columns), PLANE).reshape(slots, columns)

    score_part = dot(router, tok_all, 1, 1)
    pair_part = (score_part + swap(score_part, "c")).astype(BF)
    logits = pair_part.astype(F32) + swap(pair_part, "yh").astype(F32)
    named_all = jnp.swapaxes(slot_all.reshape(NZ, experts, rows), 0, 1).reshape(experts, NZ * rows) >= 0.0
    exponent = jnp.where(named_all, jnp.exp(logits), 0.0)
    weight_all = exponent / jnp.sum(exponent, axis=0, keepdims=True)
    weight = turned(lax.dynamic_slice_in_dim(weight_all, zi * NPLANE, NPLANE, 0), 2)
    slot_weight = jnp.sum(jnp.where(hit, weight[:, None, :], 0.0), axis=2)

    select2 = hits(quota, both).astype(BF).reshape(2, run * quota, NZ * rows)
    send_cot = lax.dot_general(select2, cot_all, (((2,), (1,)), ((0,), (0,))), preferred_element_type=F32)
    send_cot = jnp.swapaxes(send_cot.astype(BF).reshape(2, run, quota, columns), 0, 1)
    xr, send_cot, slot_weight = lax.optimization_barrier((xr, send_cot, slot_weight))
    raw = exchange(send_cot, "x").reshape(slots, columns)
    def own(a):
        return lax.dynamic_slice_in_dim(a, ci * half, half, 0)

    def other(a):
        return lax.dynamic_slice_in_dim(a, (1 - ci) * half, half, 0)

    def pair_sum(a, b, db):
        away = swap(dot(other(a), b, 1, db).astype(BF), "c")
        here = dot(own(a), b, 1, db).astype(BF)
        return (here.astype(F32) + away.astype(F32)).astype(BF)

    def swapped(pair):
        return pair, swap(pair, "yh")

    def total(pair):
        return pair[0].astype(F32) + pair[1].astype(F32)

    gate = pair_sum(xr, w_gate, 0)
    up = pair_sum(xr, w_up, 0)
    gate = swapped(gate)
    raw, gate, up = lax.optimization_barrier((raw, gate, up))
    up = swapped(up)
    away = swap(dot(other(raw), w_down, 1, 1).astype(BF), "c")
    late, up = lax.optimization_barrier((raw, up))
    here = dot(own(late), w_down, 1, 1).astype(BF)
    dh = (here.astype(F32) + away.astype(F32)).astype(BF)
    dh, slot_weight = lax.optimization_barrier((dh, slot_weight))
    slot_weight = exchange(slot_weight.reshape(NPLANE, 1, quota), PLANE).reshape(slots, 1)
    gate, up, dh = total(gate), total(up), own(slot_weight) * total(swapped(dh))
    sig = jax.nn.sigmoid(gate)
    hidden = (gate * sig * up).astype(BF)
    score = jnp.sum(dh * hidden.astype(F32), axis=1).astype(BF)
    gate_grad = (dh * up * sig * (1.0 + gate * (1.0 - sig))).astype(BF)
    up_grad = (dh * gate * sig).astype(BF)

    def whole(a):
        b = swap(a, "c")
        first = ci == 0
        return jnp.concatenate([jnp.where(first, a, b), jnp.where(first, b, a)], axis=0)

    gate_grad, up_grad, score, hidden = (whole(a) for a in (gate_grad, up_grad, score, hidden))

    back = (dot(gate_grad, w_gate, 1, 1) + dot(up_grad, w_up, 1, 1)).astype(BF)
    score = jnp.pad(score.reshape(NPLANE, 1, quota), ((0, 0), (0, MORE - 1), (0, columns - quota)))
    back = jnp.concatenate([back.reshape(NPLANE, quota, columns), score], axis=1)
    back = exchange(back, PLANE)
    grad_gate = dot(xr, gate_grad, 0, 0).astype(BF)
    grad_up = dot(xr, up_grad, 0, 0).astype(BF)
    dyw = (slot_weight * raw.astype(F32)).astype(BF)
    grad_down = dot(hidden, dyw, 0, 0).astype(BF)
    back, grad_gate, grad_up, grad_down = lax.optimization_barrier((back, grad_gate, grad_up, grad_down))
    score = back[:, quota, :quota].astype(F32)
    back = back.reshape(NPLANE * (quota + MORE), columns)
    select_back = hits(quota + MORE).astype(BF).reshape(NPLANE * (quota + MORE), NZ * rows)
    partial = dot(select_back, back, 0, 0).astype(BF)

    pair_score = jnp.sum(jnp.where(hit, score[:, :, None], 0.0), axis=1)
    row_sum = jnp.sum(pair_score, axis=0).reshape(1, NZ, rows)
    packed = jnp.concatenate(
        [
            jnp.swapaxes(pair_score.reshape(NPLANE, NZ, rows), 0, 1),
            jnp.broadcast_to(row_sum, (NZ, NZ, rows)),
        ],
        axis=1,
    )
    packed = exchange(packed, "z")
    own_score = jnp.swapaxes(packed[:, :NPLANE].reshape(NZ, run, 2, rows), 1, 2).reshape(experts, rows)
    own_weight = lax.dynamic_slice_in_dim(weight_all, zi * rows, rows, 1)
    own_grad = (own_score - own_weight * jnp.sum(own_score, axis=0, keepdims=True)).astype(BF)
    row_sum = jnp.sum(packed[:, NPLANE:], axis=0).reshape(1, NZ * rows)
    logit_grad = (pair_score - weight * row_sum).astype(BF)

    router_part = dot(logit_grad, tok_all, 1, 0)
    router_part = jnp.sum(
        exchange(jnp.broadcast_to(router_part[None], (NPLANE, NPLANE, columns)), PLANE), axis=0
    )
    router_part = turned(router_part, run)
    grad_router = exchange(jnp.broadcast_to(router_part[None], (NZ, NPLANE, columns)), "z").reshape(
        experts, columns
    )
    grad_tokens = lax.psum_scatter(partial, "z", scatter_dimension=0, tiled=True)
    grad_tokens = (grad_tokens.astype(F32) + dot(own_grad, router, 0, 0)).astype(BF)

    return grad_tokens, grad_gate[None], grad_up[None], grad_down[None], grad_router


def solution(mesh):
    fine = Mesh(mesh.devices.reshape(2, 2, NZ, 2, 4), DP + EXPERT)
    in_specs = (
        P(EXPERT, DP),
        P(EXPERT, DP),
        P(EXPERT, None),
        P(None, DP),
        P(EXPERT, DP, None),
        P(EXPERT, DP, None),
        P(EXPERT, None, DP),
    )
    out_specs = (
        P(EXPERT, DP),
        P(EXPERT, DP, None),
        P(EXPERT, DP, None),
        P(EXPERT, None, DP),
        P(None, DP),
    )
    return jax.shard_map(
        per_device, mesh=fine, in_specs=in_specs, out_specs=out_specs, check_vma=False
    )
```

```python
import jax
import jax.numpy as jnp
from jax import lax
from jax.sharding import Mesh, PartitionSpec as P

BF = jnp.bfloat16
F32 = jnp.float32
NZ = 8
NPLANE = 8
MORE = 8
DP = ("yh", "c")
EXPERT = ("z", "yl", "x")
PLANE = ("x", "yl")


def dot(a, b, da, db):
    return lax.dot_general(a, b, (((da,), (db,)), ((), ())), preferred_element_type=F32)


def shift(n, k):
    return [(i, (i + k) % n) for i in range(n)]


def swap(a, axis):
    return lax.ppermute(a, axis, [(0, 1), (1, 0)])


def exchange(a, axis):
    return lax.all_to_all(a, axis, split_axis=0, concat_axis=0, tiled=True)


def ring_gather(block, extra, zi, parts, beside):
    rows, columns = block.shape
    width = columns // parts
    whole = (jnp.zeros((NZ, rows, columns), BF), jnp.zeros((NZ, extra.shape[0], columns), BF))

    def keep(out, part, at, j):
        return (
            lax.dynamic_update_slice(out[0], part[None, :rows], (at, 0, j * width)),
            lax.dynamic_update_slice(out[1], part[None, rows:], (at, 0, j * width)),
        )

    cut = [slice(j * width, (j + 1) * width) for j in range(parts)]
    right = [jnp.concatenate([block[:, c], extra[:, c]], axis=0) for c in cut]
    left = list(right)
    for j in range(parts):
        whole = keep(whole, right[j], zi, j)
    for i in range(1, NZ // 2 + 1):
        if i == 2:
            right[0], beside = lax.optimization_barrier((right[0], beside))
        for j in range(parts):
            right[j] = lax.ppermute(right[j], "z", shift(NZ, 1))
            whole = keep(whole, right[j], (zi - i) % NZ, j)
            if i < NZ // 2:
                left[j] = lax.ppermute(left[j], "z", shift(NZ, -1))
                whole = keep(whole, left[j], (zi + i) % NZ, j)
    return whole[0].reshape(NZ * rows, columns), whole[1], beside


def per_device(tokens, cotangent, routes, router, w_gate, w_up, w_down):
    rows, columns = tokens.shape
    experts = router.shape[0]
    capacity = 9 * rows * routes.shape[1] // (8 * experts)
    quota = NZ * capacity
    slots = NPLANE * quota
    half = slots // 2
    zi, yi, ci = lax.axis_index("z"), lax.axis_index("yl"), lax.axis_index("c")
    w_gate, w_up, w_down = w_gate[0], w_up[0], w_down[0]

    def in_order(own_part, other_part):
        first = yi == 0
        return jnp.stack([jnp.where(first, own_part, other_part), jnp.where(first, other_part, own_part)])

    def turned(a, count):
        return jnp.swapaxes(a.reshape(count, -1, *a.shape[1:]), 0, 1).reshape(a.shape)

    labels = lax.broadcasted_iota(jnp.int32, (experts, rows), 0)
    named = jnp.any(routes.T[:, None, :] == labels[None], axis=0)
    before = (
        lax.broadcasted_iota(jnp.int32, (rows, rows), 0) < lax.broadcasted_iota(jnp.int32, (rows, rows), 1)
    ).astype(BF)
    slot = jnp.where(named, dot(named.astype(BF), before, 1, 0), -1.0).astype(BF)
    slot = slot.reshape(NZ, NPLANE * rows)

    cot_pair = in_order(cotangent, swap(cotangent, "yl"))
    tok_all, slot_all, cot_pair = ring_gather(tokens, slot, zi, 2, cot_pair)
    cot_all = lax.all_gather(cot_pair, "z", axis=1, tiled=True)
    slot_all = slot_all.astype(F32)
    offset = lax.broadcasted_iota(jnp.int32, (NZ, 1, 1), 0).astype(F32) * capacity
    place = lax.dynamic_slice_in_dim(slot_all, zi, 1, 1).reshape(NZ, NPLANE, rows)
    place = jnp.where(place >= 0.0, place + offset, -1.0)
    place = turned(jnp.swapaxes(place, 0, 1).reshape(NPLANE, NZ * rows), 2)

    def hits(q, place=place):
        return place[..., None, :] == lax.broadcasted_iota(jnp.int32, (1, q, 1), 1).astype(F32)

    hit = hits(quota)
    select = hit.astype(BF).reshape(slots, NZ * rows)

    run = NPLANE // 2

    def part(at):
        return lax.dynamic_index_in_dim(place.reshape(run, 2, -1), at, 1, keepdims=False)

    both = in_order(part(yi), swap(part(1 - yi), "yl"))

    send_tok = dot(select, tok_all, 1, 0).astype(BF)
    send_tok, both = lax.optimization_barrier((send_tok, both))
    xr = exchange(send_tok.reshape(NPLANE, quota, columns), PLANE).reshape(slots, columns)

    score_part = dot(router, tok_all, 1, 1)
    pair_part = (score_part + swap(score_part, "c")).astype(BF)
    other_part = swap(pair_part, "yh")
    select2 = hits(quota, both).astype(BF).reshape(2, run * quota, NZ * rows)
    send_cot = lax.dot_general(select2, cot_all, (((2,), (1,)), ((0,), (0,))), preferred_element_type=F32)
    send_cot = jnp.swapaxes(send_cot.astype(BF).reshape(2, run, quota, columns), 0, 1)
    other_part, send_cot = lax.optimization_barrier((other_part, send_cot))
    logits = pair_part.astype(F32) + other_part.astype(F32)
    named_all = jnp.swapaxes(slot_all.reshape(NZ, experts, rows), 0, 1).reshape(experts, NZ * rows) >= 0.0
    exponent = jnp.where(named_all, jnp.exp(logits), 0.0)
    weight_all = exponent / jnp.sum(exponent, axis=0, keepdims=True)
    weight = turned(lax.dynamic_slice_in_dim(weight_all, zi * NPLANE, NPLANE, 0), 2)
    slot_weight = jnp.sum(jnp.where(hit, weight[:, None, :], 0.0), axis=2)

    xr, send_cot, slot_weight = lax.optimization_barrier((xr, send_cot, slot_weight))
    raw = exchange(send_cot, "x").reshape(slots, columns)
    def own(a):
        return lax.dynamic_slice_in_dim(a, ci * half, half, 0)

    def other(a):
        return lax.dynamic_slice_in_dim(a, (1 - ci) * half, half, 0)

    def pair_sum(a, b, db):
        away = swap(dot(other(a), b, 1, db).astype(BF), "c")
        here = dot(own(a), b, 1, db).astype(BF)
        return (here.astype(F32) + away.astype(F32)).astype(BF)

    def swapped(pair):
        return pair, swap(pair, "yh")

    def total(pair):
        return pair[0].astype(F32) + pair[1].astype(F32)

    gate = pair_sum(xr, w_gate, 0)
    up = pair_sum(xr, w_up, 0)
    gate = swapped(gate)
    raw, gate, up = lax.optimization_barrier((raw, gate, up))
    up = swapped(up)
    away = swap(dot(other(raw), w_down, 1, 1).astype(BF), "c")
    late, up = lax.optimization_barrier((raw, up))
    here = dot(own(late), w_down, 1, 1).astype(BF)
    dh = (here.astype(F32) + away.astype(F32)).astype(BF)
    dh, slot_weight = lax.optimization_barrier((dh, slot_weight))
    slot_weight = exchange(slot_weight.reshape(NPLANE, 1, quota), PLANE).reshape(slots, 1)
    gate, up, dh = total(gate), total(up), own(slot_weight) * total(swapped(dh))
    sig = jax.nn.sigmoid(gate)
    hidden = (gate * sig * up).astype(BF)
    score = jnp.sum(dh * hidden.astype(F32), axis=1).astype(BF)
    gate_grad = (dh * up * sig * (1.0 + gate * (1.0 - sig))).astype(BF)
    up_grad = (dh * gate * sig).astype(BF)

    def whole(a):
        b = swap(a, "c")
        first = ci == 0
        return jnp.concatenate([jnp.where(first, a, b), jnp.where(first, b, a)], axis=0)

    gate_grad, up_grad, score, hidden = (whole(a) for a in (gate_grad, up_grad, score, hidden))

    back = (dot(gate_grad, w_gate, 1, 1) + dot(up_grad, w_up, 1, 1)).astype(BF)
    score = jnp.pad(score.reshape(NPLANE, 1, quota), ((0, 0), (0, MORE - 1), (0, columns - quota)))
    back = jnp.concatenate([back.reshape(NPLANE, quota, columns), score], axis=1)
    back = exchange(back, PLANE)
    grad_gate = dot(xr, gate_grad, 0, 0).astype(BF)
    grad_up = dot(xr, up_grad, 0, 0).astype(BF)
    dyw = (slot_weight * raw.astype(F32)).astype(BF)
    grad_down = dot(hidden, dyw, 0, 0).astype(BF)
    back, grad_gate, grad_up, grad_down = lax.optimization_barrier((back, grad_gate, grad_up, grad_down))
    score = back[:, quota, :quota].astype(F32)
    back = back.reshape(NPLANE * (quota + MORE), columns)
    select_back = hits(quota + MORE).astype(BF).reshape(NPLANE * (quota + MORE), NZ * rows)
    partial = dot(select_back, back, 0, 0).astype(BF)

    pair_score = jnp.sum(jnp.where(hit, score[:, :, None], 0.0), axis=1)
    row_sum = jnp.sum(pair_score, axis=0).reshape(1, NZ, rows)
    packed = jnp.concatenate(
        [
            jnp.swapaxes(pair_score.reshape(NPLANE, NZ, rows), 0, 1),
            jnp.broadcast_to(row_sum, (NZ, NZ, rows)),
        ],
        axis=1,
    )
    packed = exchange(packed, "z")
    own_score = jnp.swapaxes(packed[:, :NPLANE].reshape(NZ, run, 2, rows), 1, 2).reshape(experts, rows)
    own_weight = lax.dynamic_slice_in_dim(weight_all, zi * rows, rows, 1)
    own_grad = (own_score - own_weight * jnp.sum(own_score, axis=0, keepdims=True)).astype(BF)
    row_sum = jnp.sum(packed[:, NPLANE:], axis=0).reshape(1, NZ * rows)
    logit_grad = (pair_score - weight * row_sum).astype(BF)

    router_part = dot(logit_grad, tok_all, 1, 0)
    router_part = jnp.sum(
        exchange(jnp.broadcast_to(router_part[None], (NPLANE, NPLANE, columns)), PLANE), axis=0
    )
    router_part = turned(router_part, run)
    grad_router = exchange(jnp.broadcast_to(router_part[None], (NZ, NPLANE, columns)), "z").reshape(
        experts, columns
    )
    grad_tokens = lax.psum_scatter(partial, "z", scatter_dimension=0, tiled=True)
    grad_tokens = (grad_tokens.astype(F32) + dot(own_grad, router, 0, 0)).astype(BF)

    return grad_tokens, grad_gate[None], grad_up[None], grad_down[None], grad_router


def solution(mesh):
    fine = Mesh(mesh.devices.reshape(2, 2, NZ, 2, 4), DP + EXPERT)
    in_specs = (
        P(EXPERT, DP),
        P(EXPERT, DP),
        P(EXPERT, None),
        P(None, DP),
        P(EXPERT, DP, None),
        P(EXPERT, DP, None),
        P(EXPERT, None, DP),
    )
    out_specs = (
        P(EXPERT, DP),
        P(EXPERT, DP, None),
        P(EXPERT, DP, None),
        P(EXPERT, None, DP),
        P(None, DP),
    )
    return jax.shard_map(
        per_device, mesh=fine, in_specs=in_specs, out_specs=out_specs, check_vma=False
    )
```
